512 devices in a mesh: dp: 16 (over z_lo, core), tm: 32 (over x, y, z_hi).
Axes of the slice: x: 4, y: 4, z: 16 (z_hi: 2, z_lo: 8; z = z_hi * 8 + z_lo), core: 2. Of those that a mesh axis runs over, the one named last changes fastest.
Arguments:
- queries: bfloat16 [16, 8192, 1152], P('dp', 'tm'), may hold values from -96 to 96
- keys: bfloat16 [16, 8192, 1152], P('dp', 'tm'), may hold values from -6 to 6
- values: bfloat16 [16, 8192, 1152], P('dp', 'tm'), may hold values from -6 to 6
- out_grad: bfloat16 [16, 8192, 1152], P('dp', 'tm'), may hold values from -6 to 6
- lengths: int32 [16], P('dp'), may hold values from 2048 to 8192, as said below
- rel_bias: float32 [12, 768], replicated, may hold values from -4 to 4
Outputs:
- query_grad: bfloat16 [16, 8192, 1152], P('dp', 'tm')
- key_grad: bfloat16 [16, 8192, 1152], P('dp', 'tm')
- value_grad: bfloat16 [16, 8192, 1152], P('dp', 'tm')
- bias_grad: float32 [12, 768], replicated
The draws below stay inside these ranges and needn't reach their ends.
Inputs may be any that keep to these rules, and one draw needn't show every extreme that they name: Every recording's valid frames are its first lengths[r] frames; some recording is valid to its end.
All inputs are finite; a program needn't handle non-finite values.
Results may differ from the reference program's by a relative error of at most 0.007.
Values may be sent and summed in bfloat16 or wider, within the bound.
A program may use at most 128 MiB of HBM per device.

```python
import jax
import jax.numpy as jnp
from jax import lax

BLOCK = 256
HEADS = 12
HW = 1152
FRAMES = 8192
RECS = 16
OFFSETS = 768


def shared_keys(key):
    drawn = jax.random.normal(jax.random.fold_in(key, 101), (RECS, FRAMES, HW), jnp.float32)
    return jnp.clip(drawn, -6.0, 6.0)


def draw_keys(key, part):
    base_keys = shared_keys(key)
    return base_keys.astype(jnp.bfloat16)


def draw_queries(key, part):
    key = jax.random.fold_in(key, 2)
    fresh = jax.random.normal(key, (RECS, FRAMES, HW), jnp.float32)
    return jnp.clip(fresh, -96.0, 96.0).astype(jnp.bfloat16)


def draw_lengths(key, part):
    key = jax.random.fold_in(key, 3)
    drawn = jax.random.randint(key, (RECS,), FRAMES // 4, FRAMES + 1, dtype=jnp.int32)
    full_one = jax.random.randint(jax.random.fold_in(key, 1), (), 0, RECS, dtype=jnp.int32)
    return jnp.where(jnp.arange(RECS, dtype=jnp.int32) == full_one, FRAMES, drawn).astype(jnp.int32)


def shard_levels(stream_key, dims, split, low, high):
    def one(axis_at, shards_of):
        heights = jax.random.uniform(jax.random.fold_in(jax.random.fold_in(stream_key, 6), axis_at), (shards_of,), jnp.float32, low / len(split), high / len(split))
        return jnp.repeat(jnp.exp(heights), dims[axis_at] // shards_of).reshape((-1,) + (1,) * (len(dims) - axis_at - 1))

    level = one(*split[0])
    for cut in split[1:]:
        level = level * one(*cut)
    return level


def noise(rng, dims, width, bound, pieces=(), kind=jnp.bfloat16):
    factor_of = shard_levels(rng, dims, pieces, -0.22, 0.18) if pieces else 1.0
    entries = jax.random.normal(rng, dims, jnp.float32) * width * factor_of
    return jnp.minimum(jnp.maximum(entries, -bound), bound).astype(kind)


def setup_inputs(seed: int = 0) -> dict:
    seeds = jax.random.split(jax.random.key(seed), 7)
    queries = draw_queries(jax.random.fold_in(seeds[6], 71), 0)
    keys = draw_keys(jax.random.fold_in(seeds[6], 71), 0)
    values = noise(seeds[2], (RECS, FRAMES, HW), 1.0, 6.0, ((0, 16), (1, 32)))
    out_grad = noise(seeds[3], (RECS, FRAMES, HW), 1.0, 6.0, ((0, 16), (1, 32)))
    lengths = draw_lengths(jax.random.fold_in(seeds[6], 71), 0)
    rel_bias = noise(seeds[5], (HEADS, OFFSETS), 1.0, 4.0, (), jnp.float32)
    return dict(queries=queries, keys=keys, values=values, out_grad=out_grad, lengths=lengths, rel_bias=rel_bias)


masked_score = -1000000000.0

def toeplitz(vector, block_len):
    head_count = vector.shape[0]
    padded = jnp.pad(vector, ((0, 0), (0, 1)))
    repeated = jnp.broadcast_to(padded[:, None, :], (head_count, block_len, 2 * block_len))
    flattened = repeated.reshape(head_count, 2 * block_len * block_len)
    sliced = flattened[:, block_len - 1:block_len - 1 + block_len * (2 * block_len - 1)]
    return sliced.reshape(head_count, block_len, 2 * block_len - 1)[:, :, :block_len]

def diag_sums(matrix):
    head_count, block_len = (matrix.shape[0], matrix.shape[1])
    widened = jnp.pad(matrix, ((0, 0), (0, 0), (0, block_len - 1)))
    flattened = widened.reshape(head_count, block_len * (2 * block_len - 1))
    flattened = jnp.pad(flattened, ((0, 0), (block_len - 1, 1)))
    folded = flattened.reshape(head_count, block_len, 2 * block_len)
    return lax.optimization_barrier(jnp.sum(folded, axis=1))[:, :2 * block_len - 1]

def table_grad(left_sums, own_sums, block_len):
    return jnp.pad(left_sums, ((0, 0), (0, block_len + 1))) + jnp.pad(own_sums, ((0, 0), (block_len, 1)))

def rounded(array):
    return lax.optimization_barrier(array.astype(jnp.bfloat16)).astype(jnp.float32)

def reference(queries, keys, values, out_grad, lengths, rel_bias):
    record_count, frames, feature_width = queries.shape
    head_count = rel_bias.shape[0]
    head_width = feature_width // head_count
    block_len = BLOCK
    block_count = frames // block_len
    scaling = head_width ** (-0.5)
    bias_own = toeplitz(rel_bias[:, block_len:3 * block_len - 1], block_len)
    bias_left = toeplitz(rel_bias[:, :2 * block_len - 1], block_len)

    def one_record(packed):
        query_rec, key_rec, value_rec, grad_rec, length = packed
        frame_pos = jnp.arange(frames, dtype=jnp.int32)
        grad_rec = jnp.where((frame_pos < length)[:, None], grad_rec, jnp.zeros_like(grad_rec))
        shape = (block_count, block_len, head_count, head_width)
        query_blocks = query_rec.astype(jnp.float32).reshape(shape)
        key_blocks = key_rec.astype(jnp.float32).reshape(shape)
        value_blocks = value_rec.astype(jnp.float32).reshape(shape)
        grad_blocks = grad_rec.astype(jnp.float32).reshape(shape)
        zero_block = jnp.zeros((1, block_len, head_count, head_width), jnp.float32)
        key_prev = jnp.concatenate([zero_block, key_blocks[:-1]], axis=0)
        value_prev = jnp.concatenate([zero_block, value_blocks[:-1]], axis=0)
        block_ids = jnp.arange(block_count, dtype=jnp.int32)

        def one_block(items):
            query_here, key_here, key_before, value_here, value_before, grad_here, block_id = items
            own_frames = block_id * block_len + jnp.arange(block_len, dtype=jnp.int32)
            own_live = own_frames < length
            left_frames = own_frames - block_len
            left_live = (left_frames >= 0) & (left_frames < length)
            scores_own = jnp.einsum('qhe,khe->hqk', query_here, key_here) * scaling + bias_own
            scores_own = jnp.where(own_live[None, None, :], scores_own, masked_score)
            scores_left = jnp.einsum('qhe,khe->hqk', query_here, key_before) * scaling + bias_left
            scores_left = jnp.where(left_live[None, None, :], scores_left, masked_score)
            scores = jnp.concatenate([scores_left, scores_own], axis=2)
            row_top = lax.optimization_barrier(jnp.max(scores, axis=2, keepdims=True))
            expo = jnp.exp(scores - row_top)
            probs = expo / lax.optimization_barrier(jnp.sum(expo, axis=2, keepdims=True))
            value_window = jnp.concatenate([value_before, value_here], axis=0)
            dprobs = jnp.einsum('qhe,khe->hqk', grad_here, value_window)
            row_delta = lax.optimization_barrier(jnp.sum(probs * dprobs, axis=2, keepdims=True))
            dscores = probs * (dprobs - row_delta)
            probs_b = rounded(probs)
            dscores_b = rounded(dscores)
            query_grad = scaling * (jnp.einsum('hqk,khe->qhe', dscores_b[:, :, block_len:], key_here) + jnp.einsum('hqk,khe->qhe', dscores_b[:, :, :block_len], key_before))
            key_own = scaling * jnp.einsum('hqk,qhe->khe', dscores_b[:, :, block_len:], query_here)
            key_cross = rounded(scaling * jnp.einsum('hqk,qhe->khe', dscores_b[:, :, :block_len], query_here))
            value_own = jnp.einsum('hqk,qhe->khe', probs_b[:, :, block_len:], grad_here)
            value_cross = rounded(jnp.einsum('hqk,qhe->khe', probs_b[:, :, :block_len], grad_here))
            table = table_grad(diag_sums(dscores[:, :, :block_len]), diag_sums(dscores[:, :, block_len:]), block_len)
            return (query_grad, key_own, key_cross, value_own, value_cross, table)
        results = lax.map(one_block, (query_blocks, key_blocks, key_prev, value_blocks, value_prev, grad_blocks, block_ids))
        query_grad, key_own, key_cross, value_own, value_cross, tables = results
        key_next = jnp.concatenate([key_cross[1:], jnp.zeros_like(key_cross[:1])], axis=0)
        value_next = jnp.concatenate([value_cross[1:], jnp.zeros_like(value_cross[:1])], axis=0)
        query_out = query_grad.astype(jnp.bfloat16).reshape(frames, feature_width)
        key_out = (key_own + key_next).astype(jnp.bfloat16).reshape(frames, feature_width)
        value_out = (value_own + value_next).astype(jnp.bfloat16).reshape(frames, feature_width)
        return (query_out, key_out, value_out, lax.optimization_barrier(jnp.sum(tables, axis=0)))
    query_all, key_all, value_all, tables = lax.map(one_record, (queries, keys, values, out_grad, lengths))
    return (query_all, key_all, value_all, lax.optimization_barrier(jnp.sum(tables, axis=0)))
```

```python
import jax
import jax.numpy as jnp
from jax import lax
from jax.experimental import pallas as pl
from jax.experimental.pallas import tpu as pltpu
from jax.sharding import PartitionSpec as P

MESH = pl.DeviceIdType.MESH
MASKED = -1000000000.0
BLOCK = 256
HEAD = 96
GROUP = 4
WIDE = GROUP * HEAD
WINDOWS = ((0, 128), (0, 256), (128, 256), (256, 128))
SCALING = HEAD ** (-0.5)


def nt(a, b):
    return lax.dot_general(a, b, (((1,), (1,)), ((), ())), preferred_element_type=jnp.float32)


def nn(a, b):
    return jnp.dot(a, b, preferred_element_type=jnp.float32)


def head_lanes(j):
    start, width = WINDOWS[j]
    lane = lax.broadcasted_iota(jnp.int32, (1, width), 1) + start
    return ((lane >= HEAD * j) & (lane < HEAD * (j + 1))).astype(jnp.float32).astype(jnp.bfloat16)


def reverse_lanes(x):
    rows, width = x.shape
    row = lax.broadcasted_iota(jnp.int32, (128, 128), 0)
    col = lax.broadcasted_iota(jnp.int32, (128, 128), 1)
    flip = (row + col == 127).astype(jnp.float32)
    parts = [
        lax.dot_general(
            x[:, at : at + 128],
            flip,
            (((1,), (0,)), ((), ())),
            preferred_element_type=jnp.float32,
            precision=lax.Precision.HIGHEST,
        )
        for at in range(width - 128, -1, -128)
    ]
    return jnp.concatenate(parts, axis=1)


def diagonal_partials(x):
    x = jnp.concatenate([x, jnp.zeros((BLOCK, 128), jnp.float32)], axis=1)
    x = x.reshape(32, 8, 384)
    for level in range(4):
        pairs = x.reshape(x.shape[0] // 2, 2, 8, 384)
        x = pltpu.roll(pairs[:, 0], 8 << level, 2) + pairs[:, 1]
    zeros = jnp.zeros((8, 128), jnp.float32)
    return jnp.concatenate([zeros, x[0]], axis=1) + jnp.concatenate([x[1], zeros], axis=1)


def kernel(
    length_ref, q_hbm, k_hbm, v_hbm, g_hbm, rel_ref,
    dq_hbm, dk_hbm, dv_hbm, table_ref,
    qbuf, kbuf, vbuf, gbuf, ktr, rq, rg, sdq, rdq,
    expo, dpr, toep, skew, dk_acc, dv_acc, dq_tr, dq_own, gmask,
    st_send, st_recv, bk_send, bk_recv, tops, parts,
    odq, odk, odv,
    load_sem, out_sem, send_sem, recv_sem,
):
    dp = lax.axis_index("dp")
    tm = lax.axis_index("tm")
    count = lax.axis_size("tm")
    before = {"dp": dp, "tm": lax.rem(tm + count - 1, count)}
    after = {"dp": dp, "tm": lax.rem(tm + 1, count)}
    heads = rel_ref.shape[0]
    groups = heads // GROUP

    def lanes(g):
        return pl.ds(pl.multiple_of(g * WIDE, 128), WIDE)

    def remote(src, dst, kind, g, target):
        return pltpu.make_async_remote_copy(
            src_ref=src, dst_ref=dst.at[g],
            send_sem=send_sem.at[kind, g], recv_sem=recv_sem.at[kind, g],
            device_id=target, device_id_type=MESH,
        )

    def send_q(g):
        return remote(q_hbm.at[0, :, lanes(g)], rq, 0, g, before)

    def send_g(g):
        return remote(g_hbm.at[0, :, lanes(g)], rg, 1, g, before)

    def send_stats(g):
        return remote(st_send.at[g], st_recv, 2, g, before)

    def send_back(g):
        return remote(bk_send.at[g], bk_recv, 3, g, after)

    def send_dq(g):
        return remote(sdq.at[g], rdq, 4, g, after)

    def load(n, src, dst, g):
        return pltpu.make_async_copy(src.at[0, :, lanes(g)], dst.at[g], load_sem.at[n, g])

    def store(n, src, dst, g):
        return pltpu.make_async_copy(src.at[g], dst.at[0, :, lanes(g)], out_sem.at[n, g])

    loads = [
        load(n, src, dst, g)
        for g in range(groups)
        for n, (src, dst) in enumerate(((q_hbm, qbuf), (k_hbm, kbuf), (v_hbm, vbuf), (g_hbm, gbuf)))
    ]
    for copy in loads:
        copy.start()

    barrier = pltpu.get_barrier_semaphore()
    for neighbour in (before, after):
        pl.semaphore_signal(barrier, inc=1, device_id=neighbour, device_id_type=MESH)
    pl.semaphore_wait(barrier, 2)
    send_q(0).start()
    send_g(0).start()

    length = length_ref[0]
    live_keys = length - tm * BLOCK
    live_cross = jnp.where(tm == count - 1, 0, live_keys)
    live_next = jnp.where(tm == count - 1, 0, live_keys - BLOCK)

    flipped = pltpu.roll(reverse_lanes(rel_ref[...]), 3 * BLOCK - 1, 1)
    spread = jnp.broadcast_to(flipped[:, None, :], (heads, 8, 3 * BLOCK))
    sub = lax.broadcasted_iota(jnp.int32, (heads, 8, 3 * BLOCK), 1)
    for bit in (1, 2, 4):
        spread = jnp.where(((7 - sub) & bit) != 0, pltpu.roll(spread, 3 * BLOCK - bit, 2), spread)
    skew[...] = spread

    def build(h, carry):
        base = skew[h]
        for a in range(BLOCK // 8):
            shift = 8 * (BLOCK // 8 - 1 - a)
            turned = base if shift == 0 else pltpu.roll(base, 3 * BLOCK - shift, 1)
            toep[h, 8 * a : 8 * a + 8, :] = turned[:, : 2 * BLOCK]
        return carry

    lax.fori_loop(0, heads, build, 0)
    for copy in loads:
        copy.wait()

    key_row = lax.broadcasted_iota(jnp.int32, (BLOCK, BLOCK), 0)
    frame_row = lax.broadcasted_iota(jnp.int32, (BLOCK, WIDE), 0)

    def own_stats(g, carry):
        live = frame_row < live_keys
        gbuf[g] = jnp.where(live, gbuf[g].astype(jnp.float32), 0.0).astype(jnp.bfloat16)
        ktr[g] = kbuf[g].T
        for j in range(GROUP):
            h = g * GROUP + j
            start, width = WINDOWS[j]
            window = slice(start, start + width)
            mask = head_lanes(j)
            scores = nt(kbuf[g, :, window] * mask, qbuf[g, :, window]) * SCALING
            scores = scores + toep[h, :, :BLOCK]
            scores = jnp.where(key_row < live_keys, scores, MASKED)
            top = jnp.max(scores, axis=0, keepdims=True)
            e = jnp.exp(scores - top)
            dprobs = nt(vbuf[g, :, window] * mask, gbuf[g, :, window])
            total = jnp.sum(e, axis=0, keepdims=True)
            mixed = jnp.sum(e * dprobs, axis=0, keepdims=True)
            expo[h] = e
            dpr[h] = dprobs
            tops[g, j : j + 1, :] = top
            st_send[g, j : j + 1, :] = top + jnp.log(total)
            st_send[g, GROUP + j : GROUP + j + 1, :] = mixed / total
        send_stats(g).start()
        return carry

    lax.fori_loop(0, groups, own_stats, 0)
    for g in range(1, groups):
        send_q(g).start()
        send_g(g).start()

    def cross(g, carry):
        send_q(g).wait_recv()
        send_g(g).wait_recv()
        send_stats(g).wait_recv()

        @pl.when(g > 0)
        def _():
            send_dq(g - 1).start()

        gmask[...] = jnp.where(
            frame_row < live_next, rg[g].astype(jnp.float32), 0.0
        ).astype(jnp.bfloat16)
        dk_acc[g] = jnp.zeros((BLOCK, WIDE), jnp.float32)
        dv_acc[g] = jnp.zeros((BLOCK, WIDE), jnp.float32)
        for j in range(GROUP):
            h = g * GROUP + j
            start, width = WINDOWS[j]
            window = slice(start, start + width)
            mask = head_lanes(j)
            scores = nt(kbuf[g, :, window] * mask, rq[g, :, window]) * SCALING
            scores = scores + toep[h, :, BLOCK:]
            scores = jnp.where(key_row < live_cross, scores, MASKED)
            top = jnp.max(scores, axis=0, keepdims=True)
            e = jnp.exp(scores - top)
            dprobs = nt(vbuf[g, :, window] * mask, gmask[:, window])
            total = jnp.sum(e, axis=0, keepdims=True)
            mixed = jnp.sum(e * dprobs, axis=0, keepdims=True)
            lse_here = top + jnp.log(total)
            lse_there = st_recv[g, j : j + 1, :]
            highest = jnp.maximum(lse_here, lse_there)
            here = jnp.exp(lse_here - highest)
            there = jnp.exp(lse_there - highest)
            both = here + there
            lse = highest + jnp.log(both)
            delta = (here * (mixed / total) + there * st_recv[g, GROUP + j : GROUP + j + 1, :]) / both
            bk_send[g, j : j + 1, :] = lse
            bk_send[g, GROUP + j : GROUP + j + 1, :] = delta
            probs = e * jnp.exp(top - lse)
            dscores = probs * (dprobs - delta)
            probs_b = probs.astype(jnp.bfloat16)
            dscores_b = dscores.astype(jnp.bfloat16)
            dv_acc[g, :, window] += nn(probs_b, gmask[:, window] * mask)
            dk_acc[g, :, window] += nn(dscores_b, rq[g, :, window] * mask)
            dq_tr[HEAD * j : HEAD * (j + 1), :] = nn(ktr[g, HEAD * j : HEAD * (j + 1), :], dscores_b)
            parts[h, :, : BLOCK] = jnp.zeros((8, BLOCK), jnp.float32)
            parts[h, :, BLOCK:] = diagonal_partials(dscores)
        send_back(g).start()
        sdq[g] = (dq_tr[...].T * SCALING).astype(jnp.bfloat16)
        return carry

    lax.fori_loop(0, groups, cross, 0)
    send_dq(groups - 1).start()

    def own_rest(g, carry):
        send_back(g).wait_recv()
        for j in range(GROUP):
            h = g * GROUP + j
            start, width = WINDOWS[j]
            window = slice(start, start + width)
            mask = head_lanes(j)
            probs = expo[h] * jnp.exp(tops[g, j : j + 1, :] - bk_recv[g, j : j + 1, :])
            dscores = probs * (dpr[h] - bk_recv[g, GROUP + j : GROUP + j + 1, :])
            probs_b = probs.astype(jnp.bfloat16)
            dscores_b = dscores.astype(jnp.bfloat16)
            dv_acc[g, :, window] += nn(probs_b, gbuf[g, :, window] * mask)
            dk_acc[g, :, window] += nn(dscores_b, qbuf[g, :, window] * mask)
            dq_tr[HEAD * j : HEAD * (j + 1), :] = nn(ktr[g, HEAD * j : HEAD * (j + 1), :], dscores_b)
            parts[h, :, : 2 * BLOCK] += diagonal_partials(dscores)
        dq_own[g] = dq_tr[...].T * SCALING
        odk[g] = (dk_acc[g] * SCALING).astype(jnp.bfloat16)
        odv[g] = dv_acc[g].astype(jnp.bfloat16)
        store(1, odk, dk_hbm, g).start()
        store(2, odv, dv_hbm, g).start()
        return carry

    lax.fori_loop(0, groups, own_rest, 0)

    folded = parts[...]
    for bit in (1, 2, 4):
        folded = jnp.where(((7 - sub) & bit) != 0, pltpu.roll(folded, bit, 2), folded)
    sums = jnp.sum(folded, axis=1)
    table_ref[...] = pltpu.roll(reverse_lanes(sums), 3 * BLOCK - 1, 1)

    def finish(g, carry):
        send_dq(g).wait_recv()
        odq[g] = (dq_own[g] + rdq[g].astype(jnp.float32)).astype(jnp.bfloat16)
        store(0, odq, dq_hbm, g).start()
        return carry

    lax.fori_loop(0, groups, finish, 0)
    for g in range(groups):
        for copy in (send_q(g), send_g(g), send_stats(g), send_back(g), send_dq(g)):
            copy.wait_send()
        for n, (src, dst) in enumerate(((odq, dq_hbm), (odk, dk_hbm), (odv, dv_hbm))):
            store(n, src, dst, g).wait()


def per_device(queries, keys, values, out_grad, lengths, rel_bias):
    _, frames, width = queries.shape
    heads, offsets = rel_bias.shape
    groups = heads // GROUP
    bf16, f32 = jnp.bfloat16, jnp.float32
    wide = pltpu.VMEM((groups, BLOCK, WIDE), bf16)
    wide32 = pltpu.VMEM((groups, BLOCK, WIDE), f32)
    stats = pltpu.VMEM((groups, 2 * GROUP, BLOCK), f32)
    block = jax.ShapeDtypeStruct((1, frames, width), bf16)
    anywhere = pl.BlockSpec(memory_space=pl.ANY)
    in_vmem = pl.BlockSpec(memory_space=pltpu.VMEM)
    dq, dk, dv, table = pl.pallas_call(
        kernel,
        out_shape=(block, block, block, jax.ShapeDtypeStruct((heads, offsets), f32)),
        in_specs=[pl.BlockSpec(memory_space=pltpu.SMEM)] + [anywhere] * 4 + [in_vmem],
        out_specs=(anywhere, anywhere, anywhere, in_vmem),
        scratch_shapes=[
            wide, wide, wide, wide,
            pltpu.VMEM((groups, WIDE, BLOCK), bf16),
            wide, wide, wide, wide,
            pltpu.VMEM((heads, BLOCK, BLOCK), f32),
            pltpu.VMEM((heads, BLOCK, BLOCK), f32),
            pltpu.VMEM((heads, BLOCK, 2 * BLOCK), f32),
            pltpu.VMEM((heads, 8, offsets), f32),
            wide32, wide32,
            pltpu.VMEM((WIDE, BLOCK), f32),
            wide32,
            pltpu.VMEM((BLOCK, WIDE), bf16),
            stats, stats, stats, stats, stats,
            pltpu.VMEM((heads, 8, offsets), f32),
            wide, wide, wide,
            pltpu.SemaphoreType.DMA((4, groups)),
            pltpu.SemaphoreType.DMA((3, groups)),
            pltpu.SemaphoreType.DMA((5, groups)),
            pltpu.SemaphoreType.DMA((5, groups)),
        ],
        compiler_params=pltpu.CompilerParams(
            collective_id=0, has_side_effects=True, vmem_limit_bytes=48 << 20
        ),
    )(lengths, queries, keys, values, out_grad, rel_bias)
    return dq, dk, dv, lax.psum(table, ("dp", "tm"))


def solution(mesh):
    placed = P("dp", "tm", None)
    return jax.shard_map(
        per_device,
        mesh=mesh,
        in_specs=(placed, placed, placed, placed, P("dp"), P()),
        out_specs=(placed, placed, placed, P()),
        check_vma=False,
    )
```

```python
import jax
import jax.numpy as jnp
from jax import lax
from jax.experimental import pallas as pl
from jax.experimental.pallas import tpu as pltpu
from jax.sharding import PartitionSpec as P

MESH = pl.DeviceIdType.MESH
MASKED = -1000000000.0
BLOCK = 256
HEAD = 96
GROUP = 4
WIDE = GROUP * HEAD
WINDOWS = ((0, 128), (0, 256), (128, 256), (256, 128))
SCALING = HEAD ** (-0.5)
NX, NY, NZ_HI, NZ_LO, CORES = 4, 4, 2, 8, 2
NZ = NZ_HI * NZ_LO
NEAR = min(4, NZ)
FAR = NZ // NEAR


def nt(a, b):
    return lax.dot_general(a, b, (((1,), (1,)), ((), ())), preferred_element_type=jnp.float32)


def nn(a, b):
    return jnp.dot(a, b, preferred_element_type=jnp.float32)


def head_lanes(j):
    start, width = WINDOWS[j]
    lane = lax.broadcasted_iota(jnp.int32, (1, width), 1) + start
    return ((lane >= HEAD * j) & (lane < HEAD * (j + 1))).astype(jnp.float32).astype(jnp.bfloat16)


def reverse_lanes(x):
    rows, width = x.shape
    row = lax.broadcasted_iota(jnp.int32, (128, 128), 0)
    col = lax.broadcasted_iota(jnp.int32, (128, 128), 1)
    flip = (row + col == 127).astype(jnp.float32)
    parts = [
        lax.dot_general(
            x[:, at : at + 128],
            flip,
            (((1,), (0,)), ((), ())),
            preferred_element_type=jnp.float32,
            precision=lax.Precision.HIGHEST,
        )
        for at in range(width - 128, -1, -128)
    ]
    return jnp.concatenate(parts, axis=1)


def diagonal_partials(x):
    x = jnp.concatenate([x, jnp.zeros((BLOCK, 128), jnp.float32)], axis=1)
    x = x.reshape(32, 8, 384)
    for level in range(4):
        pairs = x.reshape(x.shape[0] // 2, 2, 8, 384)
        x = pltpu.roll(pairs[:, 0], 8 << level, 2) + pairs[:, 1]
    zeros = jnp.zeros((8, 128), jnp.float32)
    return jnp.concatenate([zeros, x[0]], axis=1) + jnp.concatenate([x[1], zeros], axis=1)


def place(dp, tm):
    return tm // NZ_HI // NY, tm // NZ_HI % NY, (tm % NZ_HI) * NZ_LO + dp // CORES, dp % CORES


def device(x, y, z, core):
    return {"dp": (z % NZ_LO) * CORES + core, "tm": (x * NY + y) * NZ_HI + z // NZ_LO}


def table_peers(x, y, z, core):
    base = (z // NEAR) * NEAR
    return {
        "core": [device(x, y, z, 1 - core)],
        "x": [device(lax.rem(x + r, NX), y, z, core) for r in range(1, NX)],
        "y": [device(x, lax.rem(y + r, NY), z, core) for r in range(1, NY)],
        "far": [device(x, y, lax.rem(z + r * NEAR, NZ), core) for r in range(1, FAR)],
        "near": [device(x, y, base + lax.rem(z - base + r, NEAR), core) for r in range(1, NEAR)],
    }


def kernel(
    length_ref, q_hbm, k_hbm, v_hbm, g_hbm, rel_ref,
    dq_hbm, dk_hbm, dv_hbm, table_ref,
    qbuf, kbuf, vbuf, gbuf, ktr, rq, rg, sdq, rdq,
    expo, dpr, toep, skew, dk_acc, dv_acc, dq_tr, dq_own, gmask,
    st_send, st_recv, bk_send, bk_recv, tops, parts,
    odq, odk, odv,
    halves, other, slot_x, thirds, slot_y, slot_far, slot_near, gather_y, gather,
    load_sem, out_sem, send_sem, recv_sem, sum_send, sum_recv,
):
    dp = lax.axis_index("dp")
    tm = lax.axis_index("tm")
    count = lax.axis_size("tm")
    before = {"dp": dp, "tm": lax.rem(tm + count - 1, count)}
    after = {"dp": dp, "tm": lax.rem(tm + 1, count)}
    heads = rel_ref.shape[0]
    groups = heads // GROUP

    def lanes(g):
        return pl.ds(pl.multiple_of(g * WIDE, 128), WIDE)

    def remote(src, dst, kind, g, target):
        return pltpu.make_async_remote_copy(
            src_ref=src, dst_ref=dst.at[g],
            send_sem=send_sem.at[kind, g], recv_sem=recv_sem.at[kind, g],
            device_id=target, device_id_type=MESH,
        )

    def send_q(g):
        return remote(q_hbm.at[0, :, lanes(g)], rq, 0, g, before)

    def send_g(g):
        return remote(g_hbm.at[0, :, lanes(g)], rg, 1, g, before)

    def send_stats(g):
        return remote(st_send.at[g], st_recv, 2, g, before)

    def send_back(g):
        return remote(bk_send.at[g], bk_recv, 3, g, after)

    def send_dq(g):
        return remote(sdq.at[g], rdq, 4, g, after)

    def load(n, src, dst, g):
        return pltpu.make_async_copy(src.at[0, :, lanes(g)], dst.at[g], load_sem.at[n, g])

    def store(n, src, dst, g):
        return pltpu.make_async_copy(src.at[g], dst.at[0, :, lanes(g)], out_sem.at[n, g])

    loads = [
        load(n, src, dst, g)
        for g in range(groups)
        for n, (src, dst) in enumerate(((q_hbm, qbuf), (k_hbm, kbuf), (v_hbm, vbuf), (g_hbm, gbuf)))
    ]
    for copy in loads:
        copy.start()

    barrier = pltpu.get_barrier_semaphore()
    x, y, z, core = place(dp, tm)
    peers = table_peers(x, y, z, core)
    partners = [before, after] + [peer for some in peers.values() for peer in some]
    for partner in partners:
        pl.semaphore_signal(barrier, inc=1, device_id=partner, device_id_type=MESH)
    pl.semaphore_wait(barrier, len(partners))
    send_q(0).start()
    send_g(0).start()

    length = length_ref[0]
    live_keys = length - tm * BLOCK
    live_cross = jnp.where(tm == count - 1, 0, live_keys)
    live_next = jnp.where(tm == count - 1, 0, live_keys - BLOCK)

    flipped = pltpu.roll(reverse_lanes(rel_ref[...]), 3 * BLOCK - 1, 1)
    spread = jnp.broadcast_to(flipped[:, None, :], (heads, 8, 3 * BLOCK))
    sub = lax.broadcasted_iota(jnp.int32, (heads, 8, 3 * BLOCK), 1)
    for bit in (1, 2, 4):
        spread = jnp.where(((7 - sub) & bit) != 0, pltpu.roll(spread, 3 * BLOCK - bit, 2), spread)
    skew[...] = spread

    def build(h, carry):
        base = skew[h]
        for a in range(BLOCK // 8):
            shift = 8 * (BLOCK // 8 - 1 - a)
            turned = base if shift == 0 else pltpu.roll(base, 3 * BLOCK - shift, 1)
            toep[h, 8 * a : 8 * a + 8, :] = turned[:, : 2 * BLOCK]
        return carry

    lax.fori_loop(0, heads, build, 0)
    for copy in loads:
        copy.wait()

    key_row = lax.broadcasted_iota(jnp.int32, (BLOCK, BLOCK), 0)
    frame_row = lax.broadcasted_iota(jnp.int32, (BLOCK, WIDE), 0)

    def own_stats(g, carry):
        live = frame_row < live_keys
        gbuf[g] = jnp.where(live, gbuf[g].astype(jnp.float32), 0.0).astype(jnp.bfloat16)
        ktr[g] = kbuf[g].T
        for j in range(GROUP):
            h = g * GROUP + j
            start, width = WINDOWS[j]
            window = slice(start, start + width)
            mask = head_lanes(j)
            scores = nt(kbuf[g, :, window] * mask, qbuf[g, :, window]) * SCALING
            scores = scores + toep[h, :, :BLOCK]
            scores = jnp.where(key_row < live_keys, scores, MASKED)
            top = jnp.max(scores, axis=0, keepdims=True)
            e = jnp.exp(scores - top)
            dprobs = nt(vbuf[g, :, window] * mask, gbuf[g, :, window])
            total = jnp.sum(e, axis=0, keepdims=True)
            mixed = jnp.sum(e * dprobs, axis=0, keepdims=True)
            expo[h] = e
            dpr[h] = dprobs
            tops[g, j : j + 1, :] = top
            st_send[g, j : j + 1, :] = top + jnp.log(total)
            st_send[g, GROUP + j : GROUP + j + 1, :] = mixed / total
        send_stats(g).start()
        return carry

    lax.fori_loop(0, groups, own_stats, 0)
    for g in range(1, groups):
        send_q(g).start()
        send_g(g).start()

    def cross(g, carry):
        send_q(g).wait_recv()
        send_g(g).wait_recv()
        send_stats(g).wait_recv()

        gmask[...] = jnp.where(
            frame_row < live_next, rg[g].astype(jnp.float32), 0.0
        ).astype(jnp.bfloat16)
        dk_acc[g] = jnp.zeros((BLOCK, WIDE), jnp.float32)
        dv_acc[g] = jnp.zeros((BLOCK, WIDE), jnp.float32)
        for j in range(GROUP):
            h = g * GROUP + j
            start, width = WINDOWS[j]
            window = slice(start, start + width)
            mask = head_lanes(j)
            scores = nt(kbuf[g, :, window] * mask, rq[g, :, window]) * SCALING
            scores = scores + toep[h, :, BLOCK:]
            scores = jnp.where(key_row < live_cross, scores, MASKED)
            top = jnp.max(scores, axis=0, keepdims=True)
            e = jnp.exp(scores - top)
            dprobs = nt(vbuf[g, :, window] * mask, gmask[:, window])
            total = jnp.sum(e, axis=0, keepdims=True)
            mixed = jnp.sum(e * dprobs, axis=0, keepdims=True)
            lse_here = top + jnp.log(total)
            lse_there = st_recv[g, j : j + 1, :]
            highest = jnp.maximum(lse_here, lse_there)
            here = jnp.exp(lse_here - highest)
            there = jnp.exp(lse_there - highest)
            both = here + there
            lse = highest + jnp.log(both)
            delta = (here * (mixed / total) + there * st_recv[g, GROUP + j : GROUP + j + 1, :]) / both
            bk_send[g, j : j + 1, :] = lse
            bk_send[g, GROUP + j : GROUP + j + 1, :] = delta
            probs = e * jnp.exp(top - lse)
            dscores = probs * (dprobs - delta)
            probs_b = probs.astype(jnp.bfloat16)
            dscores_b = dscores.astype(jnp.bfloat16)
            dv_acc[g, :, window] += nn(probs_b, gmask[:, window] * mask)
            dk_acc[g, :, window] += nn(dscores_b, rq[g, :, window] * mask)
            dq_tr[HEAD * j : HEAD * (j + 1), :] = nn(ktr[g, HEAD * j : HEAD * (j + 1), :], dscores_b)
            parts[h, :, : BLOCK] = jnp.zeros((8, BLOCK), jnp.float32)
            parts[h, :, BLOCK:] = diagonal_partials(dscores)
        send_back(g).start()
        sdq[g] = (dq_tr[...].T * SCALING).astype(jnp.bfloat16)
        return carry

    lax.fori_loop(0, groups, cross, 0)
    for g in range(groups):
        send_dq(g).start()

    def own_rest(g, carry):
        send_back(g).wait_recv()
        for j in range(GROUP):
            h = g * GROUP + j
            start, width = WINDOWS[j]
            window = slice(start, start + width)
            mask = head_lanes(j)
            probs = expo[h] * jnp.exp(tops[g, j : j + 1, :] - bk_recv[g, j : j + 1, :])
            dscores = probs * (dpr[h] - bk_recv[g, GROUP + j : GROUP + j + 1, :])
            probs_b = probs.astype(jnp.bfloat16)
            dscores_b = dscores.astype(jnp.bfloat16)
            dv_acc[g, :, window] += nn(probs_b, gbuf[g, :, window] * mask)
            dk_acc[g, :, window] += nn(dscores_b, qbuf[g, :, window] * mask)
            dq_tr[HEAD * j : HEAD * (j + 1), :] = nn(ktr[g, HEAD * j : HEAD * (j + 1), :], dscores_b)
            parts[h, :, : 2 * BLOCK] += diagonal_partials(dscores)
        dq_own[g] = dq_tr[...].T * SCALING
        odk[g] = (dk_acc[g] * SCALING).astype(jnp.bfloat16)
        odv[g] = dv_acc[g].astype(jnp.bfloat16)
        store(1, odk, dk_hbm, g).start()
        store(2, odv, dv_hbm, g).start()
        return carry

    lax.fori_loop(0, groups, own_rest, 0)

    folded = parts[...]
    for bit in (1, 2, 4):
        folded = jnp.where(((7 - sub) & bit) != 0, pltpu.roll(folded, bit, 2), folded)
    sums = jnp.sum(folded, axis=1)
    table = pltpu.roll(reverse_lanes(sums), 3 * BLOCK - 1, 1)

    halves[0] = table[:8]
    halves[1] = jnp.concatenate([table[8:], jnp.zeros((16 - heads, 3 * BLOCK), jnp.float32)], axis=0)

    def swap(step, targets, src, dst):
        copies = [
            pltpu.make_async_remote_copy(
                src_ref=src(r), dst_ref=dst,
                send_sem=sum_send.at[step, r], recv_sem=sum_recv.at[step, r],
                device_id=target, device_id_type=MESH,
            )
            for r, target in enumerate(targets)
        ]
        for copy in copies:
            copy.start()
        for copy in copies:
            copy.wait()

    def total(slots, count):
        value = slots[0]
        for n in range(1, count):
            value = value + slots[n]
        return value

    def swap_slots(step, targets, slots, mine, value):
        slots[mine] = value
        swap(step, targets, lambda r: slots.at[mine], slots.at[mine])

    swap(0, peers["core"], lambda r: halves.at[1 - core], other)
    swap_slots(1, peers["x"], slot_x, x, halves[core] + other[...])
    summed = total(slot_x, NX)
    for n in range(3):
        thirds[n] = summed[:, n * BLOCK : (n + 1) * BLOCK]
    slot_y[y] = thirds[jnp.minimum(y, 2)]
    swap(2, peers["y"], lambda r: thirds.at[jnp.minimum(lax.rem(y + r + 1, NY), 2)], slot_y.at[y])
    swap_slots(3, peers["far"], slot_far, z // NEAR, total(slot_y, NY))
    swap_slots(4, peers["near"], slot_near, z % NEAR, total(slot_far, FAR))
    swap_slots(5, peers["y"], gather_y, y, total(slot_near, NEAR))
    for n in range(3):
        gather[core, :, n * BLOCK : (n + 1) * BLOCK] = gather_y[n]
    swap(6, peers["core"], lambda r: gather.at[core], gather.at[core])
    table_ref[:8, :] = gather[0]
    table_ref[8:, :] = gather[1, : heads - 8, :]

    def finish(g, carry):
        send_dq(g).wait_recv()
        odq[g] = (dq_own[g] + rdq[g].astype(jnp.float32)).astype(jnp.bfloat16)
        store(0, odq, dq_hbm, g).start()
        return carry

    lax.fori_loop(0, groups, finish, 0)
    for g in range(groups):
        for copy in (send_q(g), send_g(g), send_stats(g), send_back(g), send_dq(g)):
            copy.wait_send()
        for n, (src, dst) in enumerate(((odq, dq_hbm), (odk, dk_hbm), (odv, dv_hbm))):
            store(n, src, dst, g).wait()


def per_device(queries, keys, values, out_grad, lengths, rel_bias):
    _, frames, width = queries.shape
    heads, offsets = rel_bias.shape
    groups = heads // GROUP
    bf16, f32 = jnp.bfloat16, jnp.float32
    wide = pltpu.VMEM((groups, BLOCK, WIDE), bf16)
    wide32 = pltpu.VMEM((groups, BLOCK, WIDE), f32)
    stats = pltpu.VMEM((groups, 2 * GROUP, BLOCK), f32)
    block = jax.ShapeDtypeStruct((1, frames, width), bf16)
    anywhere = pl.BlockSpec(memory_space=pl.ANY)
    in_vmem = pl.BlockSpec(memory_space=pltpu.VMEM)
    return pl.pallas_call(
        kernel,
        out_shape=(block, block, block, jax.ShapeDtypeStruct((heads, offsets), f32)),
        in_specs=[pl.BlockSpec(memory_space=pltpu.SMEM)] + [anywhere] * 4 + [in_vmem],
        out_specs=(anywhere, anywhere, anywhere, in_vmem),
        scratch_shapes=[
            wide, wide, wide, wide,
            pltpu.VMEM((groups, WIDE, BLOCK), bf16),
            wide, wide, wide, wide,
            pltpu.VMEM((heads, BLOCK, BLOCK), f32),
            pltpu.VMEM((heads, BLOCK, BLOCK), f32),
            pltpu.VMEM((heads, BLOCK, 2 * BLOCK), f32),
            pltpu.VMEM((heads, 8, offsets), f32),
            wide32, wide32,
            pltpu.VMEM((WIDE, BLOCK), f32),
            wide32,
            pltpu.VMEM((BLOCK, WIDE), bf16),
            stats, stats, stats, stats, stats,
            pltpu.VMEM((heads, 8, offsets), f32),
            wide, wide, wide,
            pltpu.VMEM((2, 8, offsets), f32),
            pltpu.VMEM((8, offsets), f32),
            pltpu.VMEM((NX, 8, offsets), f32),
            pltpu.VMEM((3, 8, BLOCK), f32),
            pltpu.VMEM((NY, 8, BLOCK), f32),
            pltpu.VMEM((FAR, 8, BLOCK), f32),
            pltpu.VMEM((NEAR, 8, BLOCK), f32),
            pltpu.VMEM((NY, 8, BLOCK), f32),
            pltpu.VMEM((2, 8, offsets), f32),
            pltpu.SemaphoreType.DMA((4, groups)),
            pltpu.SemaphoreType.DMA((3, groups)),
            pltpu.SemaphoreType.DMA((5, groups)),
            pltpu.SemaphoreType.DMA((5, groups)),
            pltpu.SemaphoreType.DMA((7, 3)),
            pltpu.SemaphoreType.DMA((7, 3)),
        ],
        compiler_params=pltpu.CompilerParams(
            collective_id=0, has_side_effects=True, vmem_limit_bytes=60 << 20
        ),
    )(lengths, queries, keys, values, out_grad, rel_bias)


def solution(mesh):
    placed = P("dp", "tm", None)
    return jax.shard_map(
        per_device,
        mesh=mesh,
        in_specs=(placed, placed, placed, placed, P("dp"), P()),
        out_specs=(placed, placed, placed, P()),
        check_vma=False,
    )
```

```python
import jax
import jax.numpy as jnp
from jax import lax
from jax.experimental import pallas as pl
from jax.experimental.pallas import tpu as pltpu
from jax.sharding import PartitionSpec as P

MESH = pl.DeviceIdType.MESH
MASKED = -1000000000.0
BLOCK = 256
HEAD = 96
GROUP = 4
WIDE = GROUP * HEAD
WINDOWS = ((0, 128), (0, 256), (128, 256), (256, 128))
SCALING = HEAD ** (-0.5)
HAND_ON = 2
NX, NY, NZ_HI, NZ_LO, CORES = 4, 4, 2, 8, 2
NZ = NZ_HI * NZ_LO
COLUMNS = NX * NY
TILES = 6


def nt(a, b):
    return lax.dot_general(a, b, (((1,), (1,)), ((), ())), preferred_element_type=jnp.float32)


def nn(a, b):
    return jnp.dot(a, b, preferred_element_type=jnp.float32)


def head_lanes(j):
    start, width = WINDOWS[j]
    lane = lax.broadcasted_iota(jnp.int32, (1, width), 1) + start
    return ((lane >= HEAD * j) & (lane < HEAD * (j + 1))).astype(jnp.float32).astype(jnp.bfloat16)


def reverse_lanes(x):
    rows, width = x.shape
    row = lax.broadcasted_iota(jnp.int32, (128, 128), 0)
    col = lax.broadcasted_iota(jnp.int32, (128, 128), 1)
    flip = (row + col == 127).astype(jnp.float32)
    parts = [
        lax.dot_general(
            x[:, at : at + 128],
            flip,
            (((1,), (0,)), ((), ())),
            preferred_element_type=jnp.float32,
            precision=lax.Precision.HIGHEST,
        )
        for at in range(width - 128, -1, -128)
    ]
    return jnp.concatenate(parts, axis=1)


def diagonal_partials(x):
    x = jnp.concatenate([x, jnp.zeros((BLOCK, 128), jnp.float32)], axis=1)
    x = x.reshape(32, 8, 384)
    for level in range(4):
        pairs = x.reshape(x.shape[0] // 2, 2, 8, 384)
        x = pltpu.roll(pairs[:, 0], 8 << level, 2) + pairs[:, 1]
    zeros = jnp.zeros((8, 128), jnp.float32)
    return jnp.concatenate([zeros, x[0]], axis=1) + jnp.concatenate([x[1], zeros], axis=1)


def place(dp, tm):
    return tm // NZ_HI // NY, tm // NZ_HI % NY, (tm % NZ_HI) * NZ_LO + dp // CORES, dp % CORES


def device(x, y, z, core):
    return {"dp": (z % NZ_LO) * CORES + core, "tm": (x * NY + y) * NZ_HI + z // NZ_LO}


def kernel(
    length_ref, q_hbm, k_hbm, v_hbm, g_hbm, rel_ref,
    dq_hbm, dk_hbm, dv_hbm, table_ref,
    qbuf, kbuf, vbuf, gbuf, glive, ktr, rq, rg, sdq, rdq,
    expo, dpr, toep, skew, dk_acc, dv_acc, dq_tr, dq_own, gmask,
    st_send, st_recv, bk_send, bk_recv, tops, parts,
    odq, odk, odv,
    halves, other, tiles, slot_xy, slot_z, gather,
    load_sem, out_sem, send_sem, recv_sem,
    core_send, core_recv, xy_send, xy_recv, z_send, z_recv, back_send, back_recv,
):
    dp = lax.axis_index("dp")
    tm = lax.axis_index("tm")
    count = lax.axis_size("tm")
    before = {"dp": dp, "tm": lax.rem(tm + count - 1, count)}
    after = {"dp": dp, "tm": lax.rem(tm + 1, count)}
    heads = rel_ref.shape[0]
    groups = heads // GROUP

    def lanes(g):
        return pl.ds(pl.multiple_of(g * WIDE, 128), WIDE)

    def remote(src, dst, kind, g, target):
        return pltpu.make_async_remote_copy(
            src_ref=src, dst_ref=dst.at[g],
            send_sem=send_sem.at[kind, g], recv_sem=recv_sem.at[kind, g],
            device_id=target, device_id_type=MESH,
        )

    def send_q(g):
        return remote(qbuf.at[g], rq, 0, g, before)

    def send_g(g):
        return remote(gbuf.at[g], rg, 1, g, before)

    def send_stats(g):
        return remote(st_send.at[g], st_recv, 2, g, before)

    def send_back(g):
        return remote(bk_send.at[g], bk_recv, 3, g, after)

    def send_dq(g):
        return remote(sdq.at[g], rdq, 4, g, after)

    def load(n, src, dst, g):
        return pltpu.make_async_copy(src.at[0, :, lanes(g)], dst.at[g], load_sem.at[n, g])

    def store(n, src, dst, g):
        return pltpu.make_async_copy(src.at[g], dst.at[0, :, lanes(g)], out_sem.at[n, g])

    loads = [
        load(n, src, dst, g)
        for g in range(groups)
        for n, (src, dst) in enumerate(((q_hbm, qbuf), (k_hbm, kbuf), (v_hbm, vbuf), (g_hbm, gbuf)))
    ]
    for copy in loads:
        copy.start()

    barrier = pltpu.get_barrier_semaphore()
    x, y, z, core = place(dp, tm)
    column = x * NY + y
    partner_core = device(x, y, z, 1 - core)
    around = [lax.rem(column + r, COLUMNS) for r in range(1, COLUMNS)]
    around = [device(other_column // NY, other_column % NY, z, core) for other_column in around]
    along = [device(x, y, lax.rem(z + r, NZ), core) for r in range(1, NZ)]
    partners = [before, after, partner_core] + around + along
    for partner in partners:
        pl.semaphore_signal(barrier, inc=1, device_id=partner, device_id_type=MESH)
    pl.semaphore_wait(barrier, len(partners))
    for n in (0, 3):
        loads[n].wait()
    send_q(0).start()
    send_g(0).start()

    length = length_ref[0]
    live_keys = length - tm * BLOCK
    live_cross = jnp.where(tm == count - 1, 0, live_keys)
    live_next = jnp.where(tm == count - 1, 0, live_keys - BLOCK)

    flipped = pltpu.roll(reverse_lanes(rel_ref[...]), 3 * BLOCK - 1, 1)
    spread = jnp.broadcast_to(flipped[:, None, :], (heads, 8, 3 * BLOCK))
    sub = lax.broadcasted_iota(jnp.int32, (heads, 8, 3 * BLOCK), 1)
    for bit in (1, 2, 4):
        spread = jnp.where(((7 - sub) & bit) != 0, pltpu.roll(spread, 3 * BLOCK - bit, 2), spread)
    skew[...] = spread

    def build(h, carry):
        base = skew[h]
        for a in range(BLOCK // 8):
            shift = 8 * (BLOCK // 8 - 1 - a)
            turned = base if shift == 0 else pltpu.roll(base, 3 * BLOCK - shift, 1)
            toep[h, 8 * a : 8 * a + 8, :] = turned[:, : 2 * BLOCK]
        return carry

    lax.fori_loop(0, heads, build, 0)
    for n, copy in enumerate(loads):
        if n not in (0, 3):
            copy.wait()

    key_row = lax.broadcasted_iota(jnp.int32, (BLOCK, BLOCK), 0)
    frame_row = lax.broadcasted_iota(jnp.int32, (BLOCK, WIDE), 0)

    def own_stats(g, carry):
        live = frame_row < live_keys
        glive[g] = jnp.where(live, gbuf[g].astype(jnp.float32), 0.0).astype(jnp.bfloat16)
        ktr[g] = kbuf[g].T
        for j in range(GROUP):
            h = g * GROUP + j
            start, width = WINDOWS[j]
            window = slice(start, start + width)
            mask = head_lanes(j)
            scores = nt(kbuf[g, :, window] * mask, qbuf[g, :, window]) * SCALING
            scores = scores + toep[h, :, :BLOCK]
            scores = jnp.where(key_row < live_keys, scores, MASKED)
            top = jnp.max(scores, axis=0, keepdims=True)
            e = jnp.exp(scores - top)
            dprobs = nt(vbuf[g, :, window] * mask, glive[g, :, window])
            total = jnp.sum(e, axis=0, keepdims=True)
            mixed = jnp.sum(e * dprobs, axis=0, keepdims=True)
            expo[h] = e
            dpr[h] = dprobs
            tops[g, j : j + 1, :] = top
            st_send[g, j : j + 1, :] = top + jnp.log(total)
            st_send[g, GROUP + j : GROUP + j + 1, :] = mixed / total
        send_stats(g).start()
        return carry

    lax.fori_loop(0, groups, own_stats, 0)
    for g in range(1, groups):
        send_q(g).start()
        send_g(g).start()

    def cross(g):
        send_q(g).wait_recv()
        send_g(g).wait_recv()
        send_stats(g).wait_recv()

        gmask[...] = jnp.where(
            frame_row < live_next, rg[g].astype(jnp.float32), 0.0
        ).astype(jnp.bfloat16)
        dk_acc[g] = jnp.zeros((BLOCK, WIDE), jnp.float32)
        dv_acc[g] = jnp.zeros((BLOCK, WIDE), jnp.float32)
        for j in range(GROUP):
            h = g * GROUP + j
            start, width = WINDOWS[j]
            window = slice(start, start + width)
            mask = head_lanes(j)
            scores = nt(kbuf[g, :, window] * mask, rq[g, :, window]) * SCALING
            scores = scores + toep[h, :, BLOCK:]
            scores = jnp.where(key_row < live_cross, scores, MASKED)
            top = jnp.max(scores, axis=0, keepdims=True)
            e = jnp.exp(scores - top)
            dprobs = nt(vbuf[g, :, window] * mask, gmask[:, window])
            total = jnp.sum(e, axis=0, keepdims=True)
            mixed = jnp.sum(e * dprobs, axis=0, keepdims=True)
            lse_here = top + jnp.log(total)
            lse_there = st_recv[g, j : j + 1, :]
            highest = jnp.maximum(lse_here, lse_there)
            here = jnp.exp(lse_here - highest)
            there = jnp.exp(lse_there - highest)
            both = here + there
            lse = highest + jnp.log(both)
            delta = (here * (mixed / total) + there * st_recv[g, GROUP + j : GROUP + j + 1, :]) / both
            bk_send[g, j : j + 1, :] = lse
            bk_send[g, GROUP + j : GROUP + j + 1, :] = delta
            probs = e * jnp.exp(top - lse)
            dscores = probs * (dprobs - delta)
            probs_b = probs.astype(jnp.bfloat16)
            dscores_b = dscores.astype(jnp.bfloat16)
            dv_acc[g, :, window] += nn(probs_b, gmask[:, window] * mask)
            dk_acc[g, :, window] += nn(dscores_b, rq[g, :, window] * mask)
            dq_tr[HEAD * j : HEAD * (j + 1), :] = nn(ktr[g, HEAD * j : HEAD * (j + 1), :], dscores_b)
            parts[h, :, : BLOCK] = jnp.zeros((8, BLOCK), jnp.float32)
            parts[h, :, BLOCK:] = diagonal_partials(dscores)
        send_back(g).start()
        sdq[g] = (dq_tr[...].T * SCALING).astype(jnp.bfloat16)

    def own_rest(g):
        send_back(g).wait_recv()
        for j in range(GROUP):
            h = g * GROUP + j
            start, width = WINDOWS[j]
            window = slice(start, start + width)
            mask = head_lanes(j)
            probs = expo[h] * jnp.exp(tops[g, j : j + 1, :] - bk_recv[g, j : j + 1, :])
            dscores = probs * (dpr[h] - bk_recv[g, GROUP + j : GROUP + j + 1, :])
            probs_b = probs.astype(jnp.bfloat16)
            dscores_b = dscores.astype(jnp.bfloat16)
            dv_acc[g, :, window] += nn(probs_b, glive[g, :, window] * mask)
            dk_acc[g, :, window] += nn(dscores_b, qbuf[g, :, window] * mask)
            dq_tr[HEAD * j : HEAD * (j + 1), :] = nn(ktr[g, HEAD * j : HEAD * (j + 1), :], dscores_b)
            parts[h, :, : 2 * BLOCK] += diagonal_partials(dscores)
        dq_own[g] = dq_tr[...].T * SCALING
        odk[g] = (dk_acc[g] * SCALING).astype(jnp.bfloat16)
        odv[g] = dv_acc[g].astype(jnp.bfloat16)
        store(1, odk, dk_hbm, g).start()
        store(2, odv, dv_hbm, g).start()

    def step(g, carry):
        @pl.when(g < groups)
        def _():
            cross(g)

        @pl.when(g == groups - 1)
        def _():
            for n in range(groups):
                send_dq(n).start()

        @pl.when(g > 0)
        def _():
            own_rest(g - 1)

        return carry

    lax.fori_loop(0, groups + 1, step, 0)

    folded = parts[...]
    for bit in (1, 2, 4):
        folded = jnp.where(((7 - sub) & bit) != 0, pltpu.roll(folded, bit, 2), folded)
    sums = jnp.sum(folded, axis=1)
    table = pltpu.roll(reverse_lanes(sums), 3 * BLOCK - 1, 1)

    padded = jnp.concatenate([table, jnp.zeros((16 - heads, 3 * BLOCK), jnp.float32)], axis=0)
    for c in range(2):
        for k in range(TILES):
            halves[c, k] = padded[8 * c : 8 * c + 8, 128 * k : 128 * k + 128]

    def move(src, dst, send, recv, target):
        return pltpu.make_async_remote_copy(
            src_ref=src, dst_ref=dst, send_sem=send, recv_sem=recv, device_id=target, device_id_type=MESH
        )

    swap = move(halves.at[1 - core], other, core_send.at[0], core_recv.at[0], partner_core)
    swap.start()
    swap.wait()
    tiles[...] = halves[core] + other[...]

    def to_owner(k):
        owner = device(k // NY, k % NY, z, core)
        return move(tiles.at[k], slot_xy.at[column], xy_send.at[k], xy_recv.at[column], owner)

    def from_column(c):
        return move(tiles.at[0], slot_xy.at[c], xy_send.at[0], xy_recv.at[c], partner_core)

    def to_z(r):
        return move(slot_z.at[z], slot_z.at[z], z_send.at[r], z_recv.at[r], along[r])

    def to_column(c):
        target = device(c // NY, c % NY, z, core)
        mine = gather.at[core, column]
        return move(mine, mine, back_send.at[c], back_recv.at[column], target)

    def from_owner(k):
        part = gather.at[core, k]
        return move(part, part, back_send.at[0], back_recv.at[k], partner_core)

    for k in range(TILES):
        @pl.when(column != k)
        def _():
            to_owner(k).start()

    @pl.when(column < TILES)
    def _():
        slot_xy[column] = tiles[column]
        for c in range(COLUMNS):
            @pl.when(column != c)
            def _():
                from_column(c).wait_recv()
        value = slot_xy[0]
        for c in range(1, COLUMNS):
            value = value + slot_xy[c]
        slot_z[z] = value
        for r in range(NZ - 1):
            to_z(r).start()
        for r in range(NZ - 1):
            to_z(r).wait()
        value = slot_z[0]
        for n in range(1, NZ):
            value = value + slot_z[n]
        gather[core, column] = value
        for c in range(COLUMNS):
            @pl.when(column != c)
            def _():
                to_column(c).start()

    for k in range(TILES):
        @pl.when(column != k)
        def _():
            from_owner(k).wait_recv()
            to_owner(k).wait_send()

    @pl.when(column < TILES)
    def _():
        for c in range(COLUMNS):
            @pl.when(column != c)
            def _():
                to_column(c).wait_send()

    swap = move(gather.at[core], gather.at[core], core_send.at[1], core_recv.at[1], partner_core)
    swap.start()
    swap.wait()
    for k in range(TILES):
        table_ref[:8, 128 * k : 128 * k + 128] = gather[0, k]
        table_ref[8:, 128 * k : 128 * k + 128] = gather[1, k, : heads - 8, :]

    def finish(g, carry):
        send_dq(g).wait_recv()
        odq[g] = (dq_own[g] + rdq[g].astype(jnp.float32)).astype(jnp.bfloat16)
        store(0, odq, dq_hbm, g).start()
        return carry

    lax.fori_loop(0, groups, finish, 0)
    for g in range(groups):
        for copy in (send_q(g), send_g(g), send_stats(g), send_back(g), send_dq(g)):
            copy.wait_send()
        for n, (src, dst) in enumerate(((odq, dq_hbm), (odk, dk_hbm), (odv, dv_hbm))):
            store(n, src, dst, g).wait()


def hand_on(dq, dk, dv, table, dq_out, dk_out, dv_out, table_out):
    dq_out[...] = dq[...]
    dk_out[...] = dk[...]
    dv_out[...] = dv[...]
    table_out[...] = table[...]


def per_device(queries, keys, values, out_grad, lengths, rel_bias):
    _, frames, width = queries.shape
    heads, offsets = rel_bias.shape
    groups = heads // GROUP
    bf16, f32 = jnp.bfloat16, jnp.float32
    wide = pltpu.VMEM((groups, BLOCK, WIDE), bf16)
    wide32 = pltpu.VMEM((groups, BLOCK, WIDE), f32)
    stats = pltpu.VMEM((groups, 2 * GROUP, BLOCK), f32)
    block = jax.ShapeDtypeStruct((1, frames, width), bf16)
    anywhere = pl.BlockSpec(memory_space=pl.ANY)
    in_vmem = pl.BlockSpec(memory_space=pltpu.VMEM)
    results = pl.pallas_call(
        kernel,
        out_shape=(block, block, block, jax.ShapeDtypeStruct((heads, offsets), f32)),
        in_specs=[pl.BlockSpec(memory_space=pltpu.SMEM)] + [anywhere] * 4 + [in_vmem],
        out_specs=(anywhere, anywhere, anywhere, in_vmem),
        scratch_shapes=[
            wide, wide, wide, wide, wide,
            pltpu.VMEM((groups, WIDE, BLOCK), bf16),
            wide, wide, wide, wide,
            pltpu.VMEM((heads, BLOCK, BLOCK), f32),
            pltpu.VMEM((heads, BLOCK, BLOCK), f32),
            pltpu.VMEM((heads, BLOCK, 2 * BLOCK), f32),
            pltpu.VMEM((heads, 8, offsets), f32),
            wide32, wide32,
            pltpu.VMEM((WIDE, BLOCK), f32),
            wide32,
            pltpu.VMEM((BLOCK, WIDE), bf16),
            stats, stats, stats, stats, stats,
            pltpu.VMEM((heads, 8, offsets), f32),
            wide, wide, wide,
            pltpu.VMEM((2, TILES, 8, 128), f32),
            pltpu.VMEM((TILES, 8, 128), f32),
            pltpu.VMEM((TILES, 8, 128), f32),
            pltpu.VMEM((COLUMNS, 8, 128), f32),
            pltpu.VMEM((NZ, 8, 128), f32),
            pltpu.VMEM((2, TILES, 8, 128), f32),
            pltpu.SemaphoreType.DMA((4, groups)),
            pltpu.SemaphoreType.DMA((3, groups)),
            pltpu.SemaphoreType.DMA((5, groups)),
            pltpu.SemaphoreType.DMA((5, groups)),
            pltpu.SemaphoreType.DMA((2,)),
            pltpu.SemaphoreType.DMA((2,)),
            pltpu.SemaphoreType.DMA((TILES,)),
            pltpu.SemaphoreType.DMA((COLUMNS,)),
            pltpu.SemaphoreType.DMA((NZ,)),
            pltpu.SemaphoreType.DMA((NZ,)),
            pltpu.SemaphoreType.DMA((COLUMNS,)),
            pltpu.SemaphoreType.DMA((TILES,)),
        ],
        compiler_params=pltpu.CompilerParams(
            collective_id=0, has_side_effects=True, vmem_limit_bytes=60 << 20
        ),
    )(lengths, queries, keys, values, out_grad, rel_bias)
    rows = pl.BlockSpec((1, frames // HAND_ON, width), lambda i: (0, i, 0))
    whole = pl.BlockSpec((heads, offsets), lambda i: (0, 0))
    return pl.pallas_call(
        hand_on,
        grid=(HAND_ON,),
        out_shape=(block, block, block, jax.ShapeDtypeStruct((heads, offsets), f32)),
        in_specs=[rows, rows, rows, whole],
        out_specs=(rows, rows, rows, whole),
        compiler_params=pltpu.CompilerParams(vmem_limit_bytes=60 << 20),
    )(*results)


def solution(mesh):
    placed = P("dp", "tm", None)
    return jax.shard_map(
        per_device,
        mesh=mesh,
        in_specs=(placed, placed, placed, placed, P("dp"), P()),
        out_specs=(placed, placed, placed, P()),
        check_vma=False,
    )
```

```python
import jax
import jax.numpy as jnp
from jax import lax
from jax.experimental import pallas as pl
from jax.experimental.pallas import tpu as pltpu
from jax.sharding import PartitionSpec as P

MESH = pl.DeviceIdType.MESH
MASKED = -1000000000.0
BLOCK = 256
HEAD = 96
GROUP = 4
WIDE = GROUP * HEAD
WINDOWS = ((0, 128), (0, 256), (128, 256), (256, 128))
SCALING = HEAD ** (-0.5)
HAND_ON = 2
NX, NY, NZ_HI, NZ_LO, CORES = 4, 4, 2, 8, 2
NZ = NZ_HI * NZ_LO
COLUMNS = NX * NY
TILES = 6


def nt(a, b):
    return lax.dot_general(a, b, (((1,), (1,)), ((), ())), preferred_element_type=jnp.float32)


def nn(a, b):
    return jnp.dot(a, b, preferred_element_type=jnp.float32)


def head_lanes(j):
    start, width = WINDOWS[j]
    lane = lax.broadcasted_iota(jnp.int32, (1, width), 1) + start
    return ((lane >= HEAD * j) & (lane < HEAD * (j + 1))).astype(jnp.float32).astype(jnp.bfloat16)


def reverse_lanes(x):
    rows, width = x.shape
    row = lax.broadcasted_iota(jnp.int32, (128, 128), 0)
    col = lax.broadcasted_iota(jnp.int32, (128, 128), 1)
    flip = (row + col == 127).astype(jnp.float32)
    parts = [
        lax.dot_general(
            x[:, at : at + 128],
            flip,
            (((1,), (0,)), ((), ())),
            preferred_element_type=jnp.float32,
            precision=lax.Precision.HIGHEST,
        )
        for at in range(width - 128, -1, -128)
    ]
    return jnp.concatenate(parts, axis=1)


def diagonal_partials(x):
    x = jnp.concatenate([x, jnp.zeros((BLOCK, 128), jnp.float32)], axis=1)
    x = x.reshape(32, 8, 384)
    for level in range(4):
        pairs = x.reshape(x.shape[0] // 2, 2, 8, 384)
        x = pltpu.roll(pairs[:, 0], 8 << level, 2) + pairs[:, 1]
    zeros = jnp.zeros((8, 128), jnp.float32)
    return jnp.concatenate([zeros, x[0]], axis=1) + jnp.concatenate([x[1], zeros], axis=1)


def place(dp, tm):
    return tm // NZ_HI // NY, tm // NZ_HI % NY, (tm % NZ_HI) * NZ_LO + dp // CORES, dp % CORES


def device(x, y, z, core):
    return {"dp": (z % NZ_LO) * CORES + core, "tm": (x * NY + y) * NZ_HI + z // NZ_LO}


def kernel(
    length_ref, q_hbm, k_hbm, v_hbm, g_hbm, rel_ref,
    dq_hbm, dk_hbm, dv_hbm, table_ref,
    qbuf, kbuf, vbuf, gbuf, glive, ktr, rq, rg, sdq, rdq,
    expo, dpr, cross_expo, cross_dpr, shift, toep, skew, dk_acc, dv_acc, dq_tr, dq_own, gmask,
    st_send, st_recv, bk_send, bk_recv, tops, parts,
    odq, odk, odv,
    halves, other, tiles, slot_xy, slot_z, gather,
    load_sem, out_sem, send_sem, recv_sem,
    core_send, core_recv, xy_send, xy_recv, z_send, z_recv, back_send, back_recv,
):
    dp = lax.axis_index("dp")
    tm = lax.axis_index("tm")
    count = lax.axis_size("tm")
    before = {"dp": dp, "tm": lax.rem(tm + count - 1, count)}
    after = {"dp": dp, "tm": lax.rem(tm + 1, count)}
    heads = rel_ref.shape[0]
    groups = heads // GROUP

    def lanes(g):
        return pl.ds(pl.multiple_of(g * WIDE, 128), WIDE)

    def remote(src, dst, kind, g, target):
        return pltpu.make_async_remote_copy(
            src_ref=src, dst_ref=dst.at[g],
            send_sem=send_sem.at[kind, g], recv_sem=recv_sem.at[kind, g],
            device_id=target, device_id_type=MESH,
        )

    def send_q(g):
        return remote(qbuf.at[g], rq, 0, g, before)

    def send_g(g):
        return remote(gbuf.at[g], rg, 1, g, before)

    def send_stats(g):
        return remote(st_send.at[g], st_recv, 2, g, before)

    def send_back(g):
        return remote(bk_send.at[g], bk_recv, 3, g, after)

    def send_dq(g):
        return remote(sdq.at[g], rdq, 4, g, after)

    def send_first(r):
        rows = pl.ds(r * (BLOCK // 2), BLOCK // 2)
        return pltpu.make_async_remote_copy(
            src_ref=sdq.at[0, rows], dst_ref=rdq.at[0, rows],
            send_sem=send_sem.at[5, r], recv_sem=recv_sem.at[5, r],
            device_id=after, device_id_type=MESH,
        )

    def load(n, src, dst, g):
        return pltpu.make_async_copy(src.at[0, :, lanes(g)], dst.at[g], load_sem.at[n, g])

    def store(n, src, dst, g):
        return pltpu.make_async_copy(src.at[g], dst.at[0, :, lanes(g)], out_sem.at[n, g])

    loads = [
        load(n, src, dst, g)
        for g in range(groups)
        for n, (src, dst) in enumerate(((q_hbm, qbuf), (k_hbm, kbuf), (v_hbm, vbuf), (g_hbm, gbuf)))
    ]
    for copy in loads:
        copy.start()

    barrier = pltpu.get_barrier_semaphore()
    x, y, z, core = place(dp, tm)
    column = x * NY + y
    partner_core = device(x, y, z, 1 - core)
    around = [lax.rem(column + r, COLUMNS) for r in range(1, COLUMNS)]
    around = [device(other_column // NY, other_column % NY, z, core) for other_column in around]
    along = [device(x, y, lax.rem(z + r, NZ), core) for r in range(1, NZ)]
    partners = [before, after, partner_core] + around + along
    for partner in partners:
        pl.semaphore_signal(barrier, inc=1, device_id=partner, device_id_type=MESH)
    pl.semaphore_wait(barrier, len(partners))
    for n in (0, 3):
        loads[n].wait()
    send_q(0).start()
    send_g(0).start()

    length = length_ref[0]
    live_keys = length - tm * BLOCK
    live_cross = jnp.where(tm == count - 1, 0, live_keys)
    live_next = jnp.where(tm == count - 1, 0, live_keys - BLOCK)

    flipped = pltpu.roll(reverse_lanes(rel_ref[...]), 3 * BLOCK - 1, 1)
    spread = jnp.broadcast_to(flipped[:, None, :], (heads, 8, 3 * BLOCK))
    sub = lax.broadcasted_iota(jnp.int32, (heads, 8, 3 * BLOCK), 1)
    for bit in (1, 2, 4):
        spread = jnp.where(((7 - sub) & bit) != 0, pltpu.roll(spread, 3 * BLOCK - bit, 2), spread)
    skew[...] = spread

    def build(h, carry):
        base = skew[h]
        for a in range(BLOCK // 8):
            shift = 8 * (BLOCK // 8 - 1 - a)
            turned = base if shift == 0 else pltpu.roll(base, 3 * BLOCK - shift, 1)
            toep[h, 8 * a : 8 * a + 8, :] = turned[:, : 2 * BLOCK]
        return carry

    lax.fori_loop(0, heads, build, 0)
    for n, copy in enumerate(loads):
        if n not in (0, 3):
            copy.wait()

    key_row = lax.broadcasted_iota(jnp.int32, (BLOCK, BLOCK), 0)
    frame_row = lax.broadcasted_iota(jnp.int32, (BLOCK, WIDE), 0)

    def own_stats(g, carry):
        live = frame_row < live_keys
        glive[g] = jnp.where(live, gbuf[g].astype(jnp.float32), 0.0).astype(jnp.bfloat16)
        ktr[g] = kbuf[g].T
        for j in range(GROUP):
            h = g * GROUP + j
            start, width = WINDOWS[j]
            window = slice(start, start + width)
            mask = head_lanes(j)
            scores = nt(kbuf[g, :, window] * mask, qbuf[g, :, window]) * SCALING
            scores = scores + toep[h, :, :BLOCK]
            scores = jnp.where(key_row < live_keys, scores, MASKED)
            top = jnp.max(scores, axis=0, keepdims=True)
            e = jnp.exp(scores - top)
            dprobs = nt(vbuf[g, :, window] * mask, glive[g, :, window])
            total = jnp.sum(e, axis=0, keepdims=True)
            mixed = jnp.sum(e * dprobs, axis=0, keepdims=True)
            expo[h] = e
            dpr[h] = dprobs
            tops[g, j : j + 1, :] = top
            st_send[g, j : j + 1, :] = top + jnp.log(total)
            st_send[g, GROUP + j : GROUP + j + 1, :] = mixed / total
        send_stats(g).start()
        return carry

    lax.fori_loop(0, groups, own_stats, 0)
    for g in range(1, groups):
        send_q(g).start()
        send_g(g).start()

    def cross(g):
        send_q(g).wait_recv()
        send_g(g).wait_recv()
        send_stats(g).wait_recv()

        gmask[...] = jnp.where(
            frame_row < live_next, rg[g].astype(jnp.float32), 0.0
        ).astype(jnp.bfloat16)
        dk_acc[g] = jnp.zeros((BLOCK, WIDE), jnp.float32)
        dv_acc[g] = jnp.zeros((BLOCK, WIDE), jnp.float32)
        for j in range(GROUP):
            h = g * GROUP + j
            start, width = WINDOWS[j]
            window = slice(start, start + width)
            mask = head_lanes(j)
            scores = nt(kbuf[g, :, window] * mask, rq[g, :, window]) * SCALING
            scores = scores + toep[h, :, BLOCK:]
            scores = jnp.where(key_row < live_cross, scores, MASKED)
            top = jnp.max(scores, axis=0, keepdims=True)
            e = jnp.exp(scores - top)
            dprobs = nt(vbuf[g, :, window] * mask, gmask[:, window])
            total = jnp.sum(e, axis=0, keepdims=True)
            mixed = jnp.sum(e * dprobs, axis=0, keepdims=True)
            lse_here = top + jnp.log(total)
            lse_there = st_recv[g, j : j + 1, :]
            highest = jnp.maximum(lse_here, lse_there)
            here = jnp.exp(lse_here - highest)
            there = jnp.exp(lse_there - highest)
            both = here + there
            lse = highest + jnp.log(both)
            delta = (here * (mixed / total) + there * st_recv[g, GROUP + j : GROUP + j + 1, :]) / both
            bk_send[g, j : j + 1, :] = lse
            bk_send[g, GROUP + j : GROUP + j + 1, :] = delta
            shift[j : j + 1, :] = top - lse
            cross_expo[j] = e
            cross_dpr[j] = dprobs
        send_back(g).start()

        @pl.when(g == groups - 1)
        def _():
            send_first(1).start()
            for n in range(1, groups - 1):
                send_dq(n).start()

        for j in range(GROUP):
            h = g * GROUP + j
            start, width = WINDOWS[j]
            window = slice(start, start + width)
            mask = head_lanes(j)
            delta = bk_send[g, GROUP + j : GROUP + j + 1, :]
            probs = cross_expo[j] * jnp.exp(shift[j : j + 1, :])
            dscores = probs * (cross_dpr[j] - delta)
            probs_b = probs.astype(jnp.bfloat16)
            dscores_b = dscores.astype(jnp.bfloat16)
            dv_acc[g, :, window] += nn(probs_b, gmask[:, window] * mask)
            dk_acc[g, :, window] += nn(dscores_b, rq[g, :, window] * mask)
            dq_tr[HEAD * j : HEAD * (j + 1), :] = nn(ktr[g, HEAD * j : HEAD * (j + 1), :], dscores_b)
            parts[h, :, : BLOCK] = jnp.zeros((8, BLOCK), jnp.float32)
            parts[h, :, BLOCK:] = diagonal_partials(dscores)
        sdq[g] = (dq_tr[...].T * SCALING).astype(jnp.bfloat16)

        @pl.when(g == 0)
        def _():
            send_first(0).start()

    def own_rest(g):
        send_back(g).wait_recv()
        for j in range(GROUP):
            h = g * GROUP + j
            start, width = WINDOWS[j]
            window = slice(start, start + width)
            mask = head_lanes(j)
            probs = expo[h] * jnp.exp(tops[g, j : j + 1, :] - bk_recv[g, j : j + 1, :])
            dscores = probs * (dpr[h] - bk_recv[g, GROUP + j : GROUP + j + 1, :])
            probs_b = probs.astype(jnp.bfloat16)
            dscores_b = dscores.astype(jnp.bfloat16)
            dv_acc[g, :, window] += nn(probs_b, glive[g, :, window] * mask)
            dk_acc[g, :, window] += nn(dscores_b, qbuf[g, :, window] * mask)
            dq_tr[HEAD * j : HEAD * (j + 1), :] = nn(ktr[g, HEAD * j : HEAD * (j + 1), :], dscores_b)
            parts[h, :, : 2 * BLOCK] += diagonal_partials(dscores)
        dq_own[g] = dq_tr[...].T * SCALING
        odk[g] = (dk_acc[g] * SCALING).astype(jnp.bfloat16)
        odv[g] = dv_acc[g].astype(jnp.bfloat16)
        store(1, odk, dk_hbm, g).start()
        store(2, odv, dv_hbm, g).start()

    def step(g, carry):
        @pl.when(g < groups)
        def _():
            cross(g)

        @pl.when(g == groups - 1)
        def _():
            send_dq(groups - 1).start()

        @pl.when(g > 0)
        def _():
            own_rest(g - 1)

        return carry

    lax.fori_loop(0, groups + 1, step, 0)

    folded = parts[...]
    for bit in (1, 2, 4):
        folded = jnp.where(((7 - sub) & bit) != 0, pltpu.roll(folded, bit, 2), folded)
    sums = jnp.sum(folded, axis=1)
    table = pltpu.roll(reverse_lanes(sums), 3 * BLOCK - 1, 1)

    padded = jnp.concatenate([table, jnp.zeros((16 - heads, 3 * BLOCK), jnp.float32)], axis=0)
    for c in range(2):
        for k in range(TILES):
            halves[c, k] = padded[8 * c : 8 * c + 8, 128 * k : 128 * k + 128]

    def move(src, dst, send, recv, target):
        return pltpu.make_async_remote_copy(
            src_ref=src, dst_ref=dst, send_sem=send, recv_sem=recv, device_id=target, device_id_type=MESH
        )

    swap = move(halves.at[1 - core], other, core_send.at[0], core_recv.at[0], partner_core)
    swap.start()
    swap.wait()
    tiles[...] = halves[core] + other[...]

    def to_owner(k):
        owner = device(k // NY, k % NY, z, core)
        return move(tiles.at[k], slot_xy.at[column], xy_send.at[k], xy_recv.at[column], owner)

    def from_column(c):
        return move(tiles.at[0], slot_xy.at[c], xy_send.at[0], xy_recv.at[c], partner_core)

    def to_z(r):
        return move(slot_z.at[z], slot_z.at[z], z_send.at[r], z_recv.at[r], along[r])

    def to_column(c):
        target = device(c // NY, c % NY, z, core)
        mine = gather.at[core, column]
        return move(mine, mine, back_send.at[c], back_recv.at[column], target)

    def from_owner(k):
        part = gather.at[core, k]
        return move(part, part, back_send.at[0], back_recv.at[k], partner_core)

    for k in range(TILES):
        @pl.when(column != k)
        def _():
            to_owner(k).start()

    @pl.when(column < TILES)
    def _():
        slot_xy[column] = tiles[column]
        for c in range(COLUMNS):
            @pl.when(column != c)
            def _():
                from_column(c).wait_recv()
        value = slot_xy[0]
        for c in range(1, COLUMNS):
            value = value + slot_xy[c]
        slot_z[z] = value
        for r in range(NZ - 1):
            to_z(r).start()
        for r in range(NZ - 1):
            to_z(r).wait()
        value = slot_z[0]
        for n in range(1, NZ):
            value = value + slot_z[n]
        gather[core, column] = value
        for c in range(COLUMNS):
            @pl.when(column != c)
            def _():
                to_column(c).start()

    for k in range(TILES):
        @pl.when(column != k)
        def _():
            from_owner(k).wait_recv()
            to_owner(k).wait_send()

    @pl.when(column < TILES)
    def _():
        for c in range(COLUMNS):
            @pl.when(column != c)
            def _():
                to_column(c).wait_send()

    swap = move(gather.at[core], gather.at[core], core_send.at[1], core_recv.at[1], partner_core)
    swap.start()
    swap.wait()
    for k in range(TILES):
        table_ref[:8, 128 * k : 128 * k + 128] = gather[0, k]
        table_ref[8:, 128 * k : 128 * k + 128] = gather[1, k, : heads - 8, :]

    def finish(g, carry):
        @pl.when(g == 0)
        def _():
            for r in range(2):
                send_first(r).wait_recv()

        @pl.when(g > 0)
        def _():
            send_dq(g).wait_recv()

        odq[g] = (dq_own[g] + rdq[g].astype(jnp.float32)).astype(jnp.bfloat16)
        store(0, odq, dq_hbm, g).start()
        return carry

    lax.fori_loop(0, groups, finish, 0)
    for g in range(groups):
        for copy in (send_q(g), send_g(g), send_stats(g), send_back(g)):
            copy.wait_send()
        for copy in (send_first(0), send_first(1)) if g == 0 else (send_dq(g),):
            copy.wait_send()
        for n, (src, dst) in enumerate(((odq, dq_hbm), (odk, dk_hbm), (odv, dv_hbm))):
            store(n, src, dst, g).wait()


def hand_on(dq, dk, dv, table, dq_out, dk_out, dv_out, table_out):
    dq_out[...] = dq[...]
    dk_out[...] = dk[...]
    dv_out[...] = dv[...]
    table_out[...] = table[...]


def per_device(queries, keys, values, out_grad, lengths, rel_bias):
    _, frames, width = queries.shape
    heads, offsets = rel_bias.shape
    groups = heads // GROUP
    bf16, f32 = jnp.bfloat16, jnp.float32
    wide = pltpu.VMEM((groups, BLOCK, WIDE), bf16)
    wide32 = pltpu.VMEM((groups, BLOCK, WIDE), f32)
    stats = pltpu.VMEM((groups, 2 * GROUP, BLOCK), f32)
    block = jax.ShapeDtypeStruct((1, frames, width), bf16)
    anywhere = pl.BlockSpec(memory_space=pl.ANY)
    in_vmem = pl.BlockSpec(memory_space=pltpu.VMEM)
    results = pl.pallas_call(
        kernel,
        out_shape=(block, block, block, jax.ShapeDtypeStruct((heads, offsets), f32)),
        in_specs=[pl.BlockSpec(memory_space=pltpu.SMEM)] + [anywhere] * 4 + [in_vmem],
        out_specs=(anywhere, anywhere, anywhere, in_vmem),
        scratch_shapes=[
            wide, wide, wide, wide, wide,
            pltpu.VMEM((groups, WIDE, BLOCK), bf16),
            wide, wide, wide, wide,
            pltpu.VMEM((heads, BLOCK, BLOCK), f32),
            pltpu.VMEM((heads, BLOCK, BLOCK), f32),
            pltpu.VMEM((GROUP, BLOCK, BLOCK), f32),
            pltpu.VMEM((GROUP, BLOCK, BLOCK), f32),
            pltpu.VMEM((2 * GROUP, BLOCK), f32),
            pltpu.VMEM((heads, BLOCK, 2 * BLOCK), f32),
            pltpu.VMEM((heads, 8, offsets), f32),
            wide32, wide32,
            pltpu.VMEM((WIDE, BLOCK), f32),
            wide32,
            pltpu.VMEM((BLOCK, WIDE), bf16),
            stats, stats, stats, stats, stats,
            pltpu.VMEM((heads, 8, offsets), f32),
            wide, wide, wide,
            pltpu.VMEM((2, TILES, 8, 128), f32),
            pltpu.VMEM((TILES, 8, 128), f32),
            pltpu.VMEM((TILES, 8, 128), f32),
            pltpu.VMEM((COLUMNS, 8, 128), f32),
            pltpu.VMEM((NZ, 8, 128), f32),
            pltpu.VMEM((2, TILES, 8, 128), f32),
            pltpu.SemaphoreType.DMA((4, groups)),
            pltpu.SemaphoreType.DMA((3, groups)),
            pltpu.SemaphoreType.DMA((6, groups)),
            pltpu.SemaphoreType.DMA((6, groups)),
            pltpu.SemaphoreType.DMA((2,)),
            pltpu.SemaphoreType.DMA((2,)),
            pltpu.SemaphoreType.DMA((TILES,)),
            pltpu.SemaphoreType.DMA((COLUMNS,)),
            pltpu.SemaphoreType.DMA((NZ,)),
            pltpu.SemaphoreType.DMA((NZ,)),
            pltpu.SemaphoreType.DMA((COLUMNS,)),
            pltpu.SemaphoreType.DMA((TILES,)),
        ],
        compiler_params=pltpu.CompilerParams(
            collective_id=0, has_side_effects=True, vmem_limit_bytes=60 << 20
        ),
    )(lengths, queries, keys, values, out_grad, rel_bias)
    rows = pl.BlockSpec((1, frames // HAND_ON, width), lambda i: (0, i, 0))
    whole = pl.BlockSpec((heads, offsets), lambda i: (0, 0))
    return pl.pallas_call(
        hand_on,
        grid=(HAND_ON,),
        out_shape=(block, block, block, jax.ShapeDtypeStruct((heads, offsets), f32)),
        in_specs=[rows, rows, rows, whole],
        out_specs=(rows, rows, rows, whole),
        compiler_params=pltpu.CompilerParams(vmem_limit_bytes=60 << 20),
    )(*results)


def solution(mesh):
    placed = P("dp", "tm", None)
    return jax.shard_map(
        per_device,
        mesh=mesh,
        in_specs=(placed, placed, placed, placed, P("dp"), P()),
        out_specs=(placed, placed, placed, P()),
        check_vma=False,
    )
```
